256 devices in a mesh: pool: 16 (over x, y), head: 16 (over z, core).
Axes of the slice: x: 4, y: 4, z: 8, core: 2. Of those that a mesh axis runs over, the one named last changes fastest.
Arguments:
- q_nope: bfloat16 [4096, 16384], P('pool', 'head'), may hold values from -6 to 6
- q_rope: bfloat16 [4096, 8192], P('pool', 'head'), may hold values from -8 to 8
- new_latent: bfloat16 [4096, 512], P('pool'), may hold values from -6 to 6
- new_rope: bfloat16 [64, 4096], P(None, 'pool'), may hold values from -8 to 8
- resident_latent: bfloat16 [16, 256, 512], P('pool'), may hold values from -6 to 6
- resident_rope: bfloat16 [16, 64, 256], P('pool'), may hold values from -6 to 6
- pool_latent: bfloat16 [512, 64, 512], P('pool'), may hold values from -6 to 6
- pool_rope: bfloat16 [512, 4096], P('pool'), may hold values from -6 to 6
- block_table: int32 [16, 32], replicated, may hold values from -1 to 511, as said below
- resident_len: int32 [16], P('pool'), may hold values from 1 to 256, as said below
- suffix_len: int32 [16], P('pool'), may hold values from 128 to 256, as said below
- w_uk: bfloat16 [128, 128, 512], P('head'), may hold values from -0.5 to 0.5
- w_uv: bfloat16 [128, 512, 128], P('head'), may hold values from -0.25 to 0.25
- w_out: bfloat16 [16384, 3584], P('head'), may hold values from -0.375 to 0.375
Outputs:
- attn_out: bfloat16 [4096, 3584], P('pool', 'head')
The draws below stay inside these ranges and needn't reach their ends.
Inputs may be any that keep to these rules, and one draw needn't show every extreme that they name: `block_table`: row s lists session s's restored blocks as pool device times 32 plus slot, in any order, then -1 entries; no block twice in the table; at most 2 blocks of one session lie on one pool device, every session has 2 on some pool device, and some session has 2 on every pool device. `resident_len`: some session has 256. `suffix_len`: some session has 256.
All inputs are finite; a program needn't handle non-finite values.
Results may differ from the reference program's by a relative error of at most 0.023.
Values may be sent and summed in bfloat16 or wider, within the bound.
A program may use at most 64 MiB of HBM per device.

```python
import jax
import jax.numpy as jnp
from jax import lax

HEADS = 128
NOPE = 128
ROPE = 64
KV = 512
VD = 128
DW = 3584
BLK = 64
CAP = 2
SUF = 256
RES = 256
SESSIONS = 16
TOKENS = 4096
SLOTS = 32
BLOCKS = 512
NBMAX = 32
N_HEAD = 16


def draw_q_rope(key, part):
    key = jax.random.fold_in(key, 11)
    base = jnp.clip(jax.random.normal(key, (TOKENS, HEADS, ROPE), jnp.float32), -6.0, 6.0)
    return base.reshape(TOKENS, HEADS * ROPE).astype(jnp.bfloat16)


def draw_new_rope(key, part):
    key = jax.random.fold_in(key, 12)
    base = jnp.clip(jax.random.normal(key, (TOKENS, ROPE), jnp.float32), -6.0, 6.0)
    return base.T.astype(jnp.bfloat16)


def draw_block_table(key, part):
    key = jax.random.fold_in(key, 21)
    key_count, key_forced, key_full, key_slots, key_order = jax.random.split(key, 5)
    counts = jax.random.randint(key_count, (SESSIONS, SESSIONS), 0, CAP + 1)
    forced = jax.random.randint(key_forced, (SESSIONS,), 0, SESSIONS)
    counts = jnp.where(jnp.arange(SESSIONS)[None, :] == forced[:, None], CAP, counts)
    full_row = jax.random.randint(key_full, (), 0, SESSIONS)
    counts = jnp.where(jnp.arange(SESSIONS)[:, None] == full_row, CAP, counts)
    slot_perm = jax.vmap(lambda inner: jax.random.permutation(inner, SLOTS))(jax.random.split(key_slots, SESSIONS))
    session_ids = jnp.arange(SESSIONS)[:, None, None]
    pool_ids = jnp.arange(SESSIONS)[None, :, None]
    block_rank = jnp.arange(CAP)[None, None, :]
    slot_of = slot_perm[pool_ids, session_ids * CAP + block_rank]
    global_ids = (pool_ids * SLOTS + slot_of).reshape(SESSIONS, NBMAX)
    live = (block_rank < counts[:, :, None]).reshape(SESSIONS, NBMAX)
    order_key = jax.vmap(lambda inner: jax.random.permutation(inner, NBMAX))(jax.random.split(key_order, SESSIONS))
    ranking = jnp.where(live, 0, NBMAX) + order_key
    order = jnp.argsort(ranking, axis=1, stable=True)
    global_ids = jnp.take_along_axis(global_ids, order, axis=1)
    live = jnp.take_along_axis(live, order, axis=1)
    return jnp.where(live, global_ids, -1).astype(jnp.int32)


def draw_resident_len(key, part):
    key = jax.random.fold_in(key, 31)
    key_len, key_top = jax.random.split(key)
    lengths = jax.random.randint(key_len, (SESSIONS,), 1, RES + 1)
    longest = jax.random.randint(key_top, (), 0, SESSIONS)
    return jnp.where(jnp.arange(SESSIONS) == longest, RES, lengths).astype(jnp.int32)


def draw_suffix_len(key, part):
    key = jax.random.fold_in(key, 41)
    key_len, key_top = jax.random.split(key)
    lengths = jax.random.randint(key_len, (SESSIONS,), SUF // 2, SUF + 1)
    longest = jax.random.randint(key_top, (), 0, SESSIONS)
    return jnp.where(jnp.arange(SESSIONS) == longest, SUF, lengths).astype(jnp.int32)


def block_levels(stream_key, dims, shards, smallest, top_value):
    def one(dim, parts):
        draws = jax.random.uniform(jax.random.fold_in(jax.random.fold_in(stream_key, 6), dim), (parts,), jnp.float32, smallest / len(shards), top_value / len(shards))
        return jnp.repeat(jnp.exp(draws), dims[dim] // parts).reshape((-1,) + (1,) * (len(dims) - dim - 1))

    gain = one(*shards[0])
    for cut in shards[1:]:
        gain = gain * one(*cut)
    return gain


def scatter_about(rng, dims, scale, limit, shards=(), held_as=jnp.bfloat16):
    level = block_levels(rng, dims, shards, -0.22, 0.18) if shards else 1.0
    drawn = jax.random.normal(rng, dims, jnp.float32) * scale * level
    return jnp.minimum(jnp.maximum(drawn, -limit), limit).astype(held_as)


def setup_inputs(seed: int = 0) -> dict:
    key_list = jax.random.split(jax.random.key(seed), 15)
    return {
        "q_nope": scatter_about(key_list[0], (TOKENS, HEADS * NOPE), 1.0, 6.0, ((0, 16), (1, 16))),
        "q_rope": draw_q_rope(jax.random.fold_in(key_list[14], 71), 0),
        "new_latent": scatter_about(key_list[2], (TOKENS, KV), 1.0, 6.0, ((0, 16),)),
        "new_rope": draw_new_rope(jax.random.fold_in(key_list[14], 71), 0),
        "resident_latent": scatter_about(key_list[4], (SESSIONS, RES, KV), 1.0, 6.0, ((0, 16),)),
        "resident_rope": scatter_about(key_list[5], (SESSIONS, ROPE, RES), 1.0, 6.0, ((0, 16),)),
        "pool_latent": scatter_about(key_list[6], (BLOCKS, BLK, KV), 1.0, 6.0, ((0, 16),)),
        "pool_rope": scatter_about(key_list[7], (BLOCKS, ROPE * BLK), 1.0, 6.0, ((0, 16),)),
        "block_table": draw_block_table(jax.random.fold_in(key_list[14], 71), 0),
        "resident_len": draw_resident_len(jax.random.fold_in(key_list[14], 71), 0),
        "suffix_len": draw_suffix_len(jax.random.fold_in(key_list[14], 71), 0),
        "w_uk": scatter_about(key_list[11], (HEADS, NOPE, KV), NOPE ** -0.5, 0.5, ((0, 16),)),
        "w_uv": scatter_about(key_list[12], (HEADS, KV, VD), KV ** -0.5, 0.25, ((0, 16),)),
        "w_out": scatter_about(key_list[13], (HEADS * VD, DW), (HEADS * VD // 64) ** -0.5, 0.375, ((0, 16),)),
    }


group_heads = 4


def attend_group(query_abs, query_rot, key_latent, key_rotary, valid, score_scale):
    scores = jnp.einsum("tgc,lc->tgl", query_abs.astype(jnp.float32), key_latent.astype(jnp.float32))
    scores = scores + jnp.einsum("tgr,rl->tgl", query_rot.astype(jnp.float32), key_rotary.astype(jnp.float32))
    scores = jnp.where(valid[:, None, :], scores * score_scale, -jnp.inf)
    row_max = jnp.max(scores, axis=2, keepdims=True)
    exp_scores = jnp.exp(scores - row_max)
    denominator = jnp.sum(exp_scores, axis=2, keepdims=True)
    weights = lax.optimization_barrier(exp_scores.astype(jnp.bfloat16)).astype(jnp.float32)
    context = jnp.einsum("tgl,lc->tgc", weights, key_latent.astype(jnp.float32))
    return (context / denominator).astype(jnp.bfloat16)


def reference(q_nope, q_rope, new_latent, new_rope, resident_latent, resident_rope, pool_latent, pool_rope, block_table, resident_len, suffix_len, w_uk, w_uv, w_out):
    score_scale = (NOPE + ROPE) ** -0.5
    positions = jnp.arange(SUF, dtype=jnp.int32)
    head_local = HEADS // N_HEAD
    groups = HEADS // group_heads
    rest_len = NBMAX * BLK

    def one_session(session):
        listed = block_table[session]
        safe_ids = jnp.maximum(listed, 0)
        rest_latent = pool_latent[safe_ids].reshape(rest_len, KV)
        rest_rotary = jnp.transpose(pool_rope[safe_ids].reshape(NBMAX, ROPE, BLK), (1, 0, 2)).reshape(ROPE, rest_len)
        rest_live = jnp.repeat(listed >= 0, BLK)
        start = (session * SUF).astype(jnp.int32)
        key_latent = jnp.concatenate([rest_latent, resident_latent[session], lax.dynamic_slice_in_dim(new_latent, start, SUF, 0)], axis=0)
        key_rotary = jnp.concatenate([rest_rotary, resident_rope[session], lax.dynamic_slice_in_dim(new_rope, start, SUF, 1)], axis=1)
        resident_live = jnp.arange(RES, dtype=jnp.int32) < resident_len[session]
        suffix_live = (positions[None, :] <= positions[:, None]) & (positions[None, :] < suffix_len[session])
        valid = jnp.concatenate([jnp.broadcast_to(rest_live[None, :], (SUF, rest_len)), jnp.broadcast_to(resident_live[None, :], (SUF, RES)), suffix_live], axis=1)
        query_nope = lax.dynamic_slice_in_dim(q_nope, start, SUF, 0).reshape(SUF, HEADS, NOPE)
        query_rot = lax.dynamic_slice_in_dim(q_rope, start, SUF, 0).reshape(SUF, HEADS, ROPE)
        query_abs = jnp.einsum("thn,hnc->thc", query_nope.astype(jnp.float32), w_uk.astype(jnp.float32)).astype(jnp.bfloat16)
        grouped_abs = jnp.transpose(query_abs.reshape(SUF, groups, group_heads, KV), (1, 0, 2, 3))
        grouped_rot = jnp.transpose(query_rot.reshape(SUF, groups, group_heads, ROPE), (1, 0, 2, 3))
        context = lax.map(lambda operands: attend_group(operands[0], operands[1], key_latent, key_rotary, valid, score_scale), (grouped_abs, grouped_rot))
        head_out = jnp.einsum("gthc,ghcv->tghv", context.astype(jnp.float32), w_uv.reshape(groups, group_heads, KV, VD).astype(jnp.float32))
        head_out = head_out.reshape(SUF, HEADS * VD).astype(jnp.bfloat16)
        shares = jnp.einsum("tgk,gkd->gtd", head_out.reshape(SUF, N_HEAD, head_local * VD).astype(jnp.float32), w_out.reshape(N_HEAD, head_local * VD, DW).astype(jnp.float32))
        shares = lax.optimization_barrier(shares.astype(jnp.bfloat16)).astype(jnp.float32)
        summed = jnp.sum(shares, axis=0)
        summed = jnp.where((positions < suffix_len[session])[:, None], summed, jnp.zeros_like(summed))
        return summed.astype(jnp.bfloat16)

    outputs = lax.map(one_session, jnp.arange(SESSIONS, dtype=jnp.int32))
    return outputs.reshape(TOKENS, DW)
```

```python
import functools
import math

import jax
import jax.numpy as jnp
from jax import lax
from jax.experimental import pallas as pl
from jax.experimental.pallas import tpu as pltpu
from jax.sharding import PartitionSpec as P

MESH = pl.DeviceIdType.MESH
NOPE = 128
ROPE = 64
KV = 512
BLK = 64
HL = 8
SUF = 256
RES = 256
SLOTS = 32
NBMAX = 32
REST = NBMAX * BLK
KEYS = REST + RES + SUF
DW = 3584
COLS = 224
NZ = 8
BIG = 1e30
FACTOR = math.log2(math.e) / math.sqrt(NOPE + ROPE)
MSG = BLK * KV // 128 + ROPE * BLK // 128
LAT = BLK * KV // 128
HALF = 128
CHUNKS = SUF // HALF
PR = HALF // 4

f32 = jnp.float32
bf16 = jnp.bfloat16


def dot(a, b):
    return jnp.dot(a, b, preferred_element_type=f32)


def kernel(
    q_nope, q_rope, new_latent, new_rope, res_latent, res_rope, pool_latent, pool_rope,
    table, res_len, suf_len, w_uk, w_uv, w_out,
    out,
    pool_l, pool_r, rope_f, send_buf, kb, loc_l, loc_r, wuk, wuv, wout, qn, qr, qx,
    kn, krm, val, ho, po, share, pair_in, right_in, left_in,
    load_sem, xy_send, z_send, c_send, kb_recv,
    pair_send, pair_recv, right_send, right_recv, left_send, left_recv,
):
    pool = lax.axis_index("pool")
    head = lax.axis_index("head")
    mx, my = pool // 4, pool % 4
    z, core = head // 2, head % 2
    zp = z % 2
    znext = lax.rem(z + 1, NZ) * 2 + core
    zprev = lax.rem(z + NZ - 1, NZ) * 2 + core
    partner = z * 2 + (1 - core)
    zkey = lax.rem(z + 1 + core * (NZ - 2), NZ) * 2 + core

    def offset_peer(o):
        dx = o // 2
        dy = 2 * (o % 2) + (dx + zp) % 2
        return ((mx + dx) % 4) * 4 + (my + dy) % 4

    loads = []

    def load(src, dst):
        copy = pltpu.make_async_copy(src, dst, load_sem.at[len(loads)])
        copy.start()
        loads.append(copy)
        return copy

    ld_pool_r = load(pool_rope, pool_r)
    ld_pool_l = load(pool_latent, pool_l)

    barrier = pltpu.get_barrier_semaphore()
    for o in range(8):
        if o == 0:
            @pl.when(zp == 1)
            def _():
                pl.semaphore_signal(barrier, inc=1, device_id=(offset_peer(0), head), device_id_type=MESH)
        else:
            pl.semaphore_signal(barrier, inc=1, device_id=(offset_peer(o), head), device_id_type=MESH)
    for other in (znext, zprev, partner):
        pl.semaphore_signal(barrier, inc=1, device_id=(pool, other), device_id_type=MESH)

    ld_res_l = load(res_latent.at[0], loc_l.at[pl.ds(0, RES)])
    ld_new_l = load(new_latent, loc_l.at[pl.ds(RES, SUF)])
    ld_uk = load(w_uk, wuk)
    ld_uv = [load(w_uv.at[h], wuv.at[:, pl.ds(h * 128, 128)]) for h in range(HL)]
    ld_res_r = load(res_rope.at[0], loc_r.at[:, pl.ds(0, RES)])
    ld_new_r = load(new_rope, loc_r.at[:, pl.ds(RES, SUF)])
    ld_qr = load(q_rope, qr)
    ld_qn = load(q_nope, qn)
    ld_out = load(w_out, wout)

    low = pool * SLOTS
    slots = []
    for o in range(8):
        row = offset_peer(o)
        found = jnp.int32(0)
        for j in range(NBMAX):
            at = j + (1 - core) * (NBMAX - 1 - 2 * j)
            rel = table[row, at] - low
            found = jnp.where((rel >= 0) & (rel < SLOTS), rel, found)
        slots.append(found)

    pick_row = lax.broadcasted_iota(jnp.int32, (16, SLOTS), 0)
    pick_lane = lax.broadcasted_iota(jnp.int32, (16, SLOTS), 1)
    pick = jnp.zeros((16, SLOTS), f32)
    for o in range(8):
        pick = jnp.where((pick_row == o) & (pick_lane == slots[o]), 1.0, pick)
    ld_pool_r.wait()
    chosen = dot(pick.astype(bf16), pool_r[...])
    for r in range(32):
        rope_f[pl.ds(r, 8, stride=32), :] = chosen[0:8, r * 128 : r * 128 + 128]
    ld_pool_l.wait()
    for o in range(8):
        block = pool_l[slots[o]]
        for j in range(4):
            send_buf[o, j * BLK : (j + 1) * BLK, :] = block[:, j * 128 : j * 128 + 128]
        send_buf[o, LAT:MSG, :] = rope_f[o * 32 : o * 32 + 32, :].astype(bf16)

    pl.semaphore_wait(barrier, 10 + zp)

    def remote(src, dst, send, recv, device):
        return pltpu.make_async_remote_copy(
            src_ref=src, dst_ref=dst, send_sem=send, recv_sem=recv,
            device_id=device, device_id_type=MESH,
        )

    def xy(o):
        return remote(send_buf.at[o], kb.at[0, 0, o], xy_send.at[o], kb_recv.at[0, 0, o], (offset_peer(o), head))

    def over_z(o):
        return remote(kb.at[0, 0, o], kb.at[1, 0, o], z_send.at[o], kb_recv.at[1, 0, o], (pool, zkey))

    def over_core(rz, o):
        return remote(kb.at[rz, 0, o], kb.at[rz, 1, o], c_send.at[rz, o], kb_recv.at[rz, 1, o], (pool, partner))

    @pl.when(zp == 1)
    def _():
        xy(0).start()

    for o in range(1, 8):
        xy(o).start()

    @pl.when(zp == 0)
    def _():
        kb[0, 0, 0] = send_buf[0]

    def arrive_xy(o):
        if o == 0:
            @pl.when(zp == 1)
            def _():
                xy(0).wait_recv()
        else:
            xy(o).wait_recv()
        over_z(o).start()
        over_core(0, o).start()

    def arrive_z(o):
        over_z(o).wait_recv()
        over_core(1, o).start()

    def arrive_core(rz, o):
        over_core(rz, o).wait_recv()

    group = lax.broadcasted_iota(jnp.int32, (16, 128), 0)
    lane = lax.broadcasted_iota(jnp.int32, (16, 128), 1)
    blk = 2 * group + lane // BLK
    b_z, b_c, b_o = blk // 16, (blk // 8) % 2, blk % 8
    b_dx = b_o // 2
    b_dy = 2 * (b_o % 2) + (b_dx + zp + b_z) % 2
    b_src = ((mx - b_dx + 4) % 4) * 4 + (my - b_dy + 4) % 4
    b_rank = (core + b_c) % 2
    b_low = b_src * SLOTS
    count = jnp.zeros((16, 128), jnp.int32)
    for j in range(NBMAX):
        listed = table[pool, j]
        count = count + jnp.where((listed >= b_low) & (listed < b_low + SLOTS), 1, 0)
    rest_bias = jnp.where(count > b_rank, 0.0, -BIG)
    first_row = lax.broadcasted_iota(jnp.int32, (64, 128), 0) == 0

    def put_bias(g, row):
        krm[64:128, g * 128 : (g + 1) * 128] = jnp.where(first_row, row, 0.0).astype(bf16)

    for g in range(16):
        put_bias(g, rest_bias[g : g + 1, :])
    lane1 = lax.broadcasted_iota(jnp.int32, (1, 128), 1)
    for g in range(4):
        limit = res_len[0] if g < 2 else suf_len[0]
        put_bias(16 + g, jnp.where(lane1 + (g % 2) * 128 < limit, 0.0, -BIG))

    def expand(lat, at, n):
        kn[:, at : at + n] = (
            lax.dot_general(
                wuk[...].reshape(HL * NOPE, KV), lat, (((1,), (1,)), ((), ())), preferred_element_type=f32
            )
            * FACTOR
        ).astype(bf16)
        val[at : at + n, :] = dot(lat, wuv[...]).astype(bf16)

    def expand_rest(rz, rc, o):
        lat = jnp.concatenate(
            [kb[rz, rc, o : o + 4, j * BLK : (j + 1) * BLK, :].reshape(4 * BLK, 128) for j in range(4)], axis=1
        )
        at = ((rz * 2 + rc) * 8 + o) * BLK
        expand(lat, at, 4 * BLK)
        for i in range(0, 4, 2):
            a = kb[rz, rc, o + i, LAT:MSG, :].astype(f32) * FACTOR
            b = kb[rz, rc, o + i + 1, LAT:MSG, :].astype(f32) * FACTOR
            even = jnp.concatenate([a[:, :BLK], b[:, :BLK]], axis=1)
            odd = jnp.concatenate([a[:, BLK:], b[:, BLK:]], axis=1)
            krm[0:64, at + i * BLK : at + (i + 2) * BLK] = jnp.concatenate([even, odd], axis=0).astype(bf16)

    ld_res_l.wait()
    ld_uk.wait()
    for copy in ld_uv:
        copy.wait()
    expand(loc_l[0:RES, :], REST, RES)
    for o in range(0, 4):
        arrive_xy(o)
    ld_new_l.wait()
    expand(loc_l[RES : RES + SUF, :], REST + RES, SUF)
    for o in range(4, 8):
        arrive_xy(o)

    ld_res_r.wait()
    ld_new_r.wait()
    perm_r = lax.broadcasted_iota(jnp.int32, (64, 64), 0)
    perm_c = lax.broadcasted_iota(jnp.int32, (64, 64), 1)
    perm = jnp.where(perm_c == 2 * (perm_r % 32) + perm_r // 32, 1.0, 0.0).astype(bf16)
    krm[0:64, REST:KEYS] = (dot(perm, loc_r[...]) * FACTOR).astype(bf16)

    expand_rest(0, 0, 0)
    for o in range(0, 4):
        arrive_z(o)
    expand_rest(0, 0, 4)
    for o in range(0, 4):
        arrive_core(0, o)
    expand_rest(0, 1, 0)
    for o in range(4, 8):
        arrive_z(o)
    for o in range(4, 8):
        arrive_core(0, o)
    expand_rest(0, 1, 4)

    ld_qr.wait()
    ld_qn.wait()
    lane_r = lax.broadcasted_iota(jnp.int32, (128, 128), 0)
    lane_c = lax.broadcasted_iota(jnp.int32, (128, 128), 1)
    one_lane = lax.broadcasted_iota(jnp.int32, (SUF, 128), 1) == 64
    for h in range(HL):
        spread = jnp.where(
            (lane_c < 64) & (lane_r == (h % 2) * 64 + 2 * (lane_c % 32) + lane_c // 32), 1.0, 0.0
        ).astype(bf16)
        turned = dot(qr[:, (h // 2) * 128 : (h // 2) * 128 + 128], spread)
        qx[h] = jnp.where(one_lane, 1.0, turned).astype(bf16)

    expand_rest(1, 0, 0)
    expand_rest(1, 0, 4)
    for o in range(0, 4):
        arrive_core(1, o)
    expand_rest(1, 1, 0)
    for o in range(4, 8):
        arrive_core(1, o)
    expand_rest(1, 1, 4)

    def pair(c):
        return remote(
            share.at[c, 1], pair_in.at[c], pair_send.at[c], pair_recv.at[c], (pool, partner)
        )

    def right(c, s):
        return remote(
            share.at[c, 0, lax.rem(z + 4 - s, NZ)], right_in.at[c, s], right_send.at[c, s],
            right_recv.at[c, s], (pool, znext),
        )

    def left(c, s):
        return remote(
            share.at[c, 0, lax.rem(z + 5 + s, NZ)], left_in.at[c, s], left_send.at[c, s],
            left_recv.at[c, s], (pool, zprev),
        )

    def ring(c, s):
        if s == 0:
            pair(c).wait_recv()
            for k in range(NZ):
                share[c, 0, k] = (share[c, 0, k].astype(f32) + pair_in[c, k].astype(f32)).astype(bf16)
        else:
            right(c, s - 1).wait_recv()
            k = lax.rem(z + 4 - s, NZ)
            share[c, 0, k] = (share[c, 0, k].astype(f32) + right_in[c, s - 1].astype(f32)).astype(bf16)
            if s < 3:
                left(c, s - 1).wait_recv()
                k = lax.rem(z + 5 + s, NZ)
                share[c, 0, k] = (share[c, 0, k].astype(f32) + left_in[c, s - 1].astype(f32)).astype(bf16)
        right(c, s).start()
        if s < 3:
            left(c, s).start()

    def finish(c):
        right(c, 3).wait_recv()
        left(c, 2).wait_recv()
        total = share[c, 0, z].astype(f32) + right_in[c, 3].astype(f32) + left_in[c, 2].astype(f32)
        for g in range(4):
            rows = lax.broadcasted_iota(jnp.int32, (PR, COLS), 0) + (c * HALF + g * PR)
            part = jnp.where(rows < suf_len[0], total[:, g * COLS : (g + 1) * COLS], 0.0)
            out[c * HALF + g * PR : c * HALF + (g + 1) * PR, :] = part.astype(bf16)

    t_row = lax.broadcasted_iota(jnp.int32, (HALF, SUF), 0)
    u_col = lax.broadcasted_iota(jnp.int32, (HALF, SUF), 1)

    def scores(c, h):
        rows = slice(c * HALF, (c + 1) * HALF)
        q = jnp.concatenate([qn[rows, h * NOPE : (h + 1) * NOPE], qx[h, rows, :]], axis=1)
        k = jnp.concatenate([kn[h * NOPE : (h + 1) * NOPE, :], krm[...]], axis=0)
        s = dot(q, k)
        own = jnp.where(u_col <= t_row + c * HALF, s[:, KEYS - SUF :], -BIG)
        return jnp.concatenate([s[:, : KEYS - SUF], own], axis=1)

    def attend(c, h, s):
        m = jnp.max(s, axis=1, keepdims=True)
        p = jnp.exp2(s - m)
        total = jnp.sum(p, axis=1, keepdims=True)
        o = dot(p.astype(bf16), val[:, h * 128 : (h + 1) * 128])
        ho[c * HALF : (c + 1) * HALF, h * 128 : (h + 1) * 128] = (o * (1.0 / total)).astype(bf16)

    for c in range(CHUNKS):
        s = scores(c, 0)
        for h in range(HL):
            later = scores(c, h + 1) if h + 1 < HL else None
            attend(c, h, s)
            s = later
            if c > 0 and h % 2 == 1:
                ring(c - 1, h // 2)
        if c == 0:
            ld_out.wait()
        for n in range(0, DW, 512):
            po[:, n : n + 512] = dot(ho[c * HALF : (c + 1) * HALF, :], wout[:, n : n + 512]).astype(bf16)
        for k in range(NZ):
            for cc in range(2):
                at = (2 * k + cc) * COLS
                share[c, (core + cc) % 2, k] = jnp.concatenate(
                    [po[g * PR : (g + 1) * PR, at : at + COLS] for g in range(4)], axis=1
                )
        pair(c).start()
        if c > 0:
            finish(c - 1)
    for s in range(4):
        ring(CHUNKS - 1, s)
    finish(CHUNKS - 1)

    @pl.when(zp == 1)
    def _():
        xy(0).wait_send()

    for o in range(8):
        if o > 0:
            xy(o).wait_send()
        over_z(o).wait_send()
        over_core(0, o).wait_send()
        over_core(1, o).wait_send()
    for c in range(CHUNKS):
        pair(c).wait_send()
        for s in range(4):
            right(c, s).wait_send()
            if s < 3:
                left(c, s).wait_send()


def body(*args):
    dma = pltpu.SemaphoreType.DMA
    vmem = lambda *shape, dtype=bf16: pltpu.VMEM(shape, dtype)
    anywhere = pl.BlockSpec(memory_space=pl.ANY)
    smem = pl.BlockSpec(memory_space=pltpu.SMEM)
    return pl.pallas_call(
        kernel,
        out_shape=jax.ShapeDtypeStruct((SUF, COLS), bf16),
        in_specs=[anywhere] * 8 + [smem] * 3 + [anywhere] * 3,
        out_specs=pl.BlockSpec(memory_space=pltpu.VMEM),
        scratch_shapes=[
            vmem(SLOTS, BLK, KV),
            vmem(SLOTS, ROPE * BLK),
            vmem(256, 128, dtype=f32),
            vmem(8, MSG, 128),
            vmem(2, 2, 8, MSG, 128),
            vmem(RES + SUF, KV),
            vmem(ROPE, RES + SUF),
            vmem(HL, NOPE, KV),
            vmem(KV, HL * 128),
            vmem(HL * 128, DW),
            vmem(SUF, HL * NOPE),
            vmem(SUF, HL * ROPE),
            vmem(HL, SUF, 128),
            vmem(HL * NOPE, KEYS),
            vmem(128, KEYS),
            vmem(KEYS, HL * 128),
            vmem(SUF, HL * 128),
            vmem(HALF, DW),
            vmem(CHUNKS, 2, NZ, PR, 4 * COLS),
            vmem(CHUNKS, NZ, PR, 4 * COLS),
            vmem(CHUNKS, 4, PR, 4 * COLS),
            vmem(CHUNKS, 3, PR, 4 * COLS),
            dma((20,)), dma((8,)), dma((8,)), dma((2, 8)), dma((2, 2, 8)),
            dma((CHUNKS,)), dma((CHUNKS,)), dma((CHUNKS, 4)), dma((CHUNKS, 4)), dma((CHUNKS, 3)), dma((CHUNKS, 3)),
        ],
        compiler_params=pltpu.CompilerParams(
            collective_id=0, has_side_effects=True, vmem_limit_bytes=60 * 2**20
        ),
        cost_estimate=pl.CostEstimate(flops=12 * 10**9, bytes_accessed=14 * 10**6, transcendentals=5 * 10**6),
    )(*args)


def solution(mesh):
    placed = (
        P("pool", "head"), P("pool", "head"), P("pool", None), P(None, "pool"),
        P("pool", None, None), P("pool", None, None), P("pool", None, None), P("pool", None),
        P(), P("pool"), P("pool"),
        P("head", None, None), P("head", None, None), P("head", None),
    )
    return jax.shard_map(
        body, mesh=mesh, in_specs=placed, out_specs=P("pool", "head"), check_vma=False
    )
```

```python
import functools
import math

import jax
import jax.numpy as jnp
from jax import lax
from jax.experimental import pallas as pl
from jax.experimental.pallas import tpu as pltpu
from jax.sharding import PartitionSpec as P

MESH = pl.DeviceIdType.MESH
NOPE = 128
ROPE = 64
KV = 512
BLK = 64
HL = 8
SUF = 256
RES = 256
SLOTS = 32
NBMAX = 32
REST = NBMAX * BLK
KEYS = REST + RES + SUF
DW = 3584
COLS = 224
NZ = 8
BIG = 1e30
FACTOR = math.log2(math.e) / math.sqrt(NOPE + ROPE)
MSG = BLK * KV // 128 + ROPE * BLK // 128
LAT = BLK * KV // 128
HALF = 128
CHUNKS = SUF // HALF
PR = HALF // 4
MINE = ((1, 2), (2, 3), (3, 3))
BOTH = ((2, 2), (2, 0), (0, 2), (1, 3), (3, 1), (1, 0), (3, 0), (0, 1), (0, 3))
OFFSETS = MINE + ((0, 0),) + BOTH
SENT = len(OFFSETS)
OWN = 3
EARLY = 2
SPLIT = (8 - EARLY) * 4 * BLK

f32 = jnp.float32
bf16 = jnp.bfloat16


def dot(a, b):
    return jnp.dot(a, b, preferred_element_type=f32)


def kernel(
    q_nope, q_rope, new_latent, new_rope, res_latent, res_rope, pool_latent, pool_rope,
    table, res_len, suf_len, w_uk, w_uv, w_out,
    out,
    pool_l, pool_r, rope_f, send_buf, kb, loc_l, loc_r, wuk, wuv, wout, qn, qr, qx,
    kn, krm, val, o_early, m_early, l_early, ho, po, share, pair_in, sums_in,
    load_sem, xy_send, z_send, c_send, kb_recv,
    pair_send, pair_recv, sums_send, sums_recv,
):
    pool = lax.axis_index("pool")
    head = lax.axis_index("head")
    mx, my = pool // 4, pool % 4
    z, core = head // 2, head % 2
    zp = z % 2
    partner = z * 2 + (1 - core)

    def along_z(n):
        return lax.rem(z + NZ + n, NZ) * 2 + core

    zkey = lax.rem(z + 1 + core * (NZ - 2), NZ) * 2 + core

    def peer(o, way):
        dx, dy = OFFSETS[o]
        if o < OWN:
            way = way * (1 - 2 * zp)
        return ((mx + way * dx + 4) % 4) * 4 + (my + way * dy + 4) % 4

    loads = []

    def load(src, dst):
        copy = pltpu.make_async_copy(src, dst, load_sem.at[len(loads)])
        copy.start()
        loads.append(copy)
        return copy

    ld_pool_r = load(pool_rope, pool_r)
    ld_pool_l = load(pool_latent, pool_l)

    barrier = pltpu.get_barrier_semaphore()
    for o in range(SENT):
        if o != OWN:
            pl.semaphore_signal(barrier, inc=1, device_id=(peer(o, -1), head), device_id_type=MESH)
    for other in (partner, along_z(1), along_z(-1), along_z(2), along_z(-2)):
        pl.semaphore_signal(barrier, inc=1, device_id=(pool, other), device_id_type=MESH)

    ld_res_l = load(res_latent.at[0], loc_l.at[pl.ds(0, RES)])
    ld_new_l = load(new_latent, loc_l.at[pl.ds(RES, SUF)])
    ld_uk = load(w_uk, wuk)
    ld_uv = [load(w_uv.at[h], wuv.at[:, pl.ds(h * 128, 128)]) for h in range(HL)]
    ld_res_r = load(res_rope.at[0], loc_r.at[:, pl.ds(0, RES)])
    ld_new_r = load(new_rope, loc_r.at[:, pl.ds(RES, SUF)])
    ld_qr = load(q_rope, qr)
    ld_qn = load(q_nope, qn)
    ld_out = load(w_out, wout)

    low = pool * SLOTS
    slots = []
    for o in range(SENT):
        row = peer(o, 1)
        found = jnp.int32(0)
        for j in range(NBMAX):
            at = j + (1 - core) * (NBMAX - 1 - 2 * j)
            rel = table[row, at] - low
            found = jnp.where((rel >= 0) & (rel < SLOTS), rel, found)
        slots.append(found)

    pick_row = lax.broadcasted_iota(jnp.int32, (16, SLOTS), 0)
    pick_lane = lax.broadcasted_iota(jnp.int32, (16, SLOTS), 1)
    pick = jnp.zeros((16, SLOTS), f32)
    for o in range(SENT):
        pick = jnp.where((pick_row == o) & (pick_lane == slots[o]), 1.0, pick)
    ld_pool_r.wait()
    chosen = dot(pick.astype(bf16), pool_r[...])
    for r in range(32):
        rope_f[pl.ds(r, 16, stride=32), :] = chosen[:, r * 128 : r * 128 + 128]
    ld_pool_l.wait()
    for o in range(SENT):
        block = pool_l[slots[o]]
        for j in range(4):
            send_buf[o, j * BLK : (j + 1) * BLK, :] = block[:, j * 128 : j * 128 + 128]
        send_buf[o, LAT:MSG, :] = rope_f[o * 32 : o * 32 + 32, :].astype(bf16)
    kb[0, OWN] = send_buf[OWN]

    pl.semaphore_wait(barrier, SENT - 1 + 5)

    def remote(src, dst, send, recv, device):
        return pltpu.make_async_remote_copy(
            src_ref=src, dst_ref=dst, send_sem=send, recv_sem=recv,
            device_id=device, device_id_type=MESH,
        )

    def xy(o):
        return remote(send_buf.at[o], kb.at[0, o], xy_send.at[o], kb_recv.at[0, o], (peer(o, 1), head))

    def over_z(o):
        return remote(kb.at[0, o], kb.at[0, SENT + o], z_send.at[o], kb_recv.at[0, SENT + o], (pool, zkey))

    def over_core(o):
        return remote(kb.at[0, o], kb.at[1, o], c_send.at[o], kb_recv.at[1, o], (pool, partner))

    def arrive(*which):
        for o in which:
            if o >= SENT:
                over_z(o - SENT).wait_recv()
            elif o != OWN:
                xy(o).wait_recv()
            if o < OWN:
                over_z(o).start()
            over_core(o).start()

    def arrive_core(*which):
        for o in which:
            over_core(o).wait_recv()

    def send(*which):
        for o in which:
            xy(o).start()

    def left(*which):
        for o in which:
            xy(o).wait_send()

    send(0, 1, 2, 4, 5, 6)
    over_core(OWN).start()

    group = lax.broadcasted_iota(jnp.int32, (16, 128), 0)
    lane = lax.broadcasted_iota(jnp.int32, (16, 128), 1)
    blk = 2 * group + lane // BLK
    turn = 7 - blk // 4
    b_c, b_o = turn % 2, (turn // 2) * 4 + blk % 4
    b_dx, b_dy = jnp.zeros_like(blk), jnp.zeros_like(blk)
    for o in range(16):
        dx, dy = OFFSETS[o] if o < SENT else OFFSETS[o - SENT]
        way = (1 - 2 * zp) if o < OWN else (2 * zp - 1) if o >= SENT else 1
        b_dx = jnp.where(b_o == o, dx * way, b_dx)
        b_dy = jnp.where(b_o == o, dy * way, b_dy)
    b_src = ((mx - b_dx + 4) % 4) * 4 + (my - b_dy + 4) % 4
    b_rank = (core + b_c) % 2
    b_low = b_src * SLOTS
    count = jnp.zeros((16, 128), jnp.int32)
    for j in range(NBMAX):
        listed = table[pool, j]
        count = count + jnp.where((listed >= b_low) & (listed < b_low + SLOTS), 1, 0)
    rest_bias = jnp.where(count > b_rank, 0.0, -BIG)
    first_row = lax.broadcasted_iota(jnp.int32, (64, 128), 0) == 0

    def put_bias(g, row):
        krm[64:128, g * 128 : (g + 1) * 128] = jnp.where(first_row, row, 0.0).astype(bf16)

    for g in range(16):
        put_bias(g, rest_bias[g : g + 1, :])
    lane1 = lax.broadcasted_iota(jnp.int32, (1, 128), 1)
    for g in range(4):
        limit = res_len[0] if g < 2 else suf_len[0]
        put_bias(16 + g, jnp.where(lane1 + (g % 2) * 128 < limit, 0.0, -BIG))

    def expand(lat, at, n):
        kn[:, at : at + n] = (
            lax.dot_general(
                wuk[...].reshape(HL * NOPE, KV), lat, (((1,), (1,)), ((), ())), preferred_element_type=f32
            )
            * FACTOR
        ).astype(bf16)
        val[at : at + n, :] = dot(lat, wuv[...]).astype(bf16)

    def expand_rest(rc, o):
        lat = jnp.concatenate(
            [kb[rc, o : o + 4, j * BLK : (j + 1) * BLK, :].reshape(4 * BLK, 128) for j in range(4)], axis=1
        )
        at = (7 - (o // 4 * 2 + rc)) * 4 * BLK
        expand(lat, at, 4 * BLK)
        for i in range(0, 4, 2):
            a = kb[rc, o + i, LAT:MSG, :].astype(f32) * FACTOR
            b = kb[rc, o + i + 1, LAT:MSG, :].astype(f32) * FACTOR
            even = jnp.concatenate([a[:, :BLK], b[:, :BLK]], axis=1)
            odd = jnp.concatenate([a[:, BLK:], b[:, BLK:]], axis=1)
            krm[0:64, at + i * BLK : at + (i + 2) * BLK] = jnp.concatenate([even, odd], axis=0).astype(bf16)

    t_row = lax.broadcasted_iota(jnp.int32, (SUF, SUF), 0)
    u_col = lax.broadcasted_iota(jnp.int32, (SUF, SUF), 1)

    def scores(rows, h, keys):
        q = jnp.concatenate([qn[rows, h * NOPE : (h + 1) * NOPE], qx[h, rows, :]], axis=1)
        k = jnp.concatenate([kn[h * NOPE : (h + 1) * NOPE, keys], krm[:, keys]], axis=0)
        return dot(q, k)

    early = slice(SPLIT, KEYS)
    late = slice(0, SPLIT)

    def early_scores(h):
        s = scores(slice(0, SUF), h, early)
        n = KEYS - SUF - SPLIT
        return jnp.concatenate([s[:, :n], jnp.where(u_col <= t_row, s[:, n:], -BIG)], axis=1)

    def attend_early(h, s):
        m = jnp.max(s, axis=1, keepdims=True)
        p = jnp.exp2(s - m)
        total = jnp.sum(p, axis=1, keepdims=True)
        o_early[h] = dot(p.astype(bf16), val[early, h * 128 : (h + 1) * 128])
        m_early[h] = jnp.broadcast_to(m, (SUF, 128))
        l_early[h] = jnp.broadcast_to(total, (SUF, 128))

    def attend(c, h, s):
        rows = slice(c * HALF, (c + 1) * HALF)
        m0 = m_early[h, rows, :]
        m = jnp.maximum(m0, jnp.max(s, axis=1, keepdims=True))
        old = jnp.exp2(m0 - m)
        p = jnp.exp2(s - m[:, 0:1])
        total = l_early[h, rows, :] * old + jnp.sum(p, axis=1, keepdims=True)
        o = o_early[h, rows, :] * old + dot(p.astype(bf16), val[late, h * 128 : (h + 1) * 128])
        ho[rows, h * 128 : (h + 1) * 128] = (o / total).astype(bf16)

    def early_heads(first, last):
        s = early_scores(first)
        for h in range(first, last):
            later = early_scores(h + 1) if h + 1 < last else None
            attend_early(h, s)
            s = later

    ld_res_l.wait()
    ld_uk.wait()
    for copy in ld_uv:
        copy.wait()
    expand(loc_l[0:RES, :], REST, RES)
    left(0, 1, 2)
    send(7, 8, 9)
    ld_new_l.wait()
    expand(loc_l[RES : RES + SUF, :], REST + RES, SUF)
    arrive(0, 1, 2)
    left(4, 5, 6)
    send(10, 11, 12)

    ld_res_r.wait()
    ld_new_r.wait()
    perm_r = lax.broadcasted_iota(jnp.int32, (64, 64), 0)
    perm_c = lax.broadcasted_iota(jnp.int32, (64, 64), 1)
    perm = jnp.where(perm_c == 2 * (perm_r % 32) + perm_r // 32, 1.0, 0.0).astype(bf16)
    krm[0:64, REST:KEYS] = (dot(perm, loc_r[...]) * FACTOR).astype(bf16)

    ld_qr.wait()
    ld_qn.wait()
    lane_r = lax.broadcasted_iota(jnp.int32, (128, 128), 0)
    lane_c = lax.broadcasted_iota(jnp.int32, (128, 128), 1)
    one_lane = lax.broadcasted_iota(jnp.int32, (SUF, 128), 1) == 64
    for h in range(HL):
        spread = jnp.where(
            (lane_c < 64) & (lane_r == (h % 2) * 64 + 2 * (lane_c % 32) + lane_c // 32), 1.0, 0.0
        ).astype(bf16)
        turned = dot(qr[:, (h // 2) * 128 : (h // 2) * 128 + 128], spread)
        qx[h] = jnp.where(one_lane, 1.0, turned).astype(bf16)

    expand_rest(0, 0)
    arrive(4, 5, 6, 7)
    arrive_core(0, 1, 2, OWN)
    expand_rest(1, 0)
    early_heads(0, 3)
    arrive(8, 9, 10, 11)
    expand_rest(0, 4)
    early_heads(3, 6)
    arrive(12, 13, 14, 15)
    arrive_core(4, 5, 6, 7)
    expand_rest(1, 4)
    early_heads(6, 8)
    expand_rest(0, 8)
    arrive_core(8, 9, 10, 11)
    expand_rest(1, 8)
    expand_rest(0, 12)
    arrive_core(12, 13, 14, 15)
    expand_rest(1, 12)

    def pair(c):
        return remote(
            share.at[c, 1], pair_in.at[c], pair_send.at[c], pair_recv.at[c], (pool, partner)
        )

    def hop(c, i):
        way = 1 - 2 * (c % 2)
        of, to = ((4, 2 * way), (3, 1), (-3, -1), (1, 1), (-1, -1), (2, 2), (-2, -2))[i]
        return remote(
            share.at[c, 0, lax.rem(z + NZ + of, NZ)], sums_in.at[c, i], sums_send.at[c, i],
            sums_recv.at[c, i], (pool, along_z(to)),
        )

    def add(c, of, *parts):
        k = lax.rem(z + NZ + of, NZ)
        total = share[c, 0, k].astype(f32)
        for part in parts:
            total = total + part.astype(f32)
        share[c, 0, k] = total.astype(bf16)

    def paired(c, *which):
        for of in which:
            add(c, of, pair_in[c, lax.rem(z + NZ + of, NZ)])

    def step1(c):
        pair(c).wait_recv()
        paired(c, 4, 3, -3)
        for i in range(3):
            hop(c, i).start()
        paired(c, 1, -1)
        for i in range(3, 5):
            hop(c, i).start()
        paired(c, 2, -2, 0)

    def step2(c):
        for i in range(3):
            hop(c, i).wait_recv()
        if c % 2 == 0:
            add(c, 2, sums_in[c, 0], sums_in[c, 1])
            add(c, -2, sums_in[c, 2])
        else:
            add(c, 2, sums_in[c, 1])
            add(c, -2, sums_in[c, 0], sums_in[c, 2])
        for i in range(5, 7):
            hop(c, i).start()

    def finish(c):
        for i in range(3, 7):
            hop(c, i).wait_recv()
        total = share[c, 0, z].astype(f32)
        for i in range(3, 7):
            total = total + sums_in[c, i].astype(f32)
        for g in range(4):
            rows = lax.broadcasted_iota(jnp.int32, (PR, COLS), 0) + (c * HALF + g * PR)
            part = jnp.where(rows < suf_len[0], total[:, g * COLS : (g + 1) * COLS], 0.0)
            out[c * HALF + g * PR : c * HALF + (g + 1) * PR, :] = part.astype(bf16)

    for c in range(CHUNKS):
        rows = slice(c * HALF, (c + 1) * HALF)
        s = scores(rows, 0, late)
        for h in range(HL):
            later = scores(rows, h + 1, late) if h + 1 < HL else None
            attend(c, h, s)
            s = later
            if c > 0 and h == 4:
                step1(c - 1)
        if c == 0:
            ld_out.wait()
        for n in range(0, DW, 512):
            po[:, n : n + 512] = dot(ho[c * HALF : (c + 1) * HALF, :], wout[:, n : n + 512]).astype(bf16)
        for k in range(NZ):
            for cc in range(2):
                at = (2 * k + cc) * COLS
                share[c, (core + cc) % 2, k] = jnp.concatenate(
                    [po[g * PR : (g + 1) * PR, at : at + COLS] for g in range(4)], axis=1
                )
        pair(c).start()
    step1(1)
    step2(0)
    step2(1)
    finish(0)
    finish(1)

    left(7, 8, 9, 10, 11, 12)
    for o in range(OWN):
        over_z(o).wait_send()
    for o in range(16):
        over_core(o).wait_send()
    for c in range(CHUNKS):
        pair(c).wait_send()
        for i in range(7):
            hop(c, i).wait_send()


def body(*args):
    dma = pltpu.SemaphoreType.DMA
    vmem = lambda *shape, dtype=bf16: pltpu.VMEM(shape, dtype)
    anywhere = pl.BlockSpec(memory_space=pl.ANY)
    smem = pl.BlockSpec(memory_space=pltpu.SMEM)
    return pl.pallas_call(
        kernel,
        out_shape=jax.ShapeDtypeStruct((SUF, COLS), bf16),
        in_specs=[anywhere] * 8 + [smem] * 3 + [anywhere] * 3,
        out_specs=pl.BlockSpec(memory_space=pltpu.VMEM),
        scratch_shapes=[
            vmem(SLOTS, BLK, KV),
            vmem(SLOTS, ROPE * BLK),
            vmem(16 * 32, 128, dtype=f32),
            vmem(SENT, MSG, 128),
            vmem(2, 16, MSG, 128),
            vmem(RES + SUF, KV),
            vmem(ROPE, RES + SUF),
            vmem(HL, NOPE, KV),
            vmem(KV, HL * 128),
            vmem(HL * 128, DW),
            vmem(SUF, HL * NOPE),
            vmem(SUF, HL * ROPE),
            vmem(HL, SUF, 128),
            vmem(HL * NOPE, KEYS),
            vmem(128, KEYS),
            vmem(KEYS, HL * 128),
            vmem(HL, SUF, 128, dtype=f32),
            vmem(HL, SUF, 128, dtype=f32),
            vmem(HL, SUF, 128, dtype=f32),
            vmem(SUF, HL * 128),
            vmem(HALF, DW),
            vmem(CHUNKS, 2, NZ, PR, 4 * COLS),
            vmem(CHUNKS, NZ, PR, 4 * COLS),
            vmem(CHUNKS, 7, PR, 4 * COLS),
            dma((20,)), dma((SENT,)), dma((OWN,)), dma((16,)), dma((2, 16)),
            dma((CHUNKS,)), dma((CHUNKS,)), dma((CHUNKS, 7)), dma((CHUNKS, 7)),
        ],
        compiler_params=pltpu.CompilerParams(
            collective_id=0, has_side_effects=True, vmem_limit_bytes=60 * 2**20
        ),
        cost_estimate=pl.CostEstimate(flops=12 * 10**9, bytes_accessed=14 * 10**6, transcendentals=5 * 10**6),
    )(*args)


def solution(mesh):
    placed = (
        P("pool", "head"), P("pool", "head"), P("pool", None), P(None, "pool"),
        P("pool", None, None), P("pool", None, None), P("pool", None, None), P("pool", None),
        P(), P("pool"), P("pool"),
        P("head", None, None), P("head", None, None), P("head", None),
    )
    return jax.shard_map(
        body, mesh=mesh, in_specs=placed, out_specs=P("pool", "head"), check_vma=False
    )
```

```python
import functools
import math

import jax
import jax.numpy as jnp
from jax import lax
from jax.experimental import pallas as pl
from jax.experimental.pallas import tpu as pltpu
from jax.sharding import PartitionSpec as P

MESH = pl.DeviceIdType.MESH
NOPE = 128
ROPE = 64
KV = 512
BLK = 64
HL = 8
SUF = 256
RES = 256
SLOTS = 32
NBMAX = 32
REST = NBMAX * BLK
KEYS = REST + RES + SUF
DW = 3584
COLS = 224
NZ = 8
BIG = 1e30
FACTOR = math.log2(math.e) / math.sqrt(NOPE + ROPE)
MSG = BLK * KV // 128 + ROPE * BLK // 128
LAT = BLK * KV // 128
HALF = 128
CHUNKS = SUF // HALF
PR = HALF // 4
MINE = ((1, 2), (2, 3), (3, 3))
BOTH = ((2, 2), (2, 0), (0, 2), (1, 3), (3, 1), (1, 0), (3, 0), (0, 1), (0, 3))
OFFSETS = MINE + ((0, 0),) + BOTH
SENT = len(OFFSETS)
OWN = 3
EARLY = 2
SPLIT = (8 - EARLY) * 4 * BLK

f32 = jnp.float32
bf16 = jnp.bfloat16


def dot(a, b):
    return jnp.dot(a, b, preferred_element_type=f32)


def kernel(
    q_nope, q_rope, new_latent, new_rope, res_latent, res_rope, pool_latent, pool_rope,
    table, res_len, suf_len, w_uk, w_uv, w_out,
    out,
    pool_l, pool_r, rope_f, send_buf, kb, loc_l, loc_r, wuk, wuv, wout, qn, qr, qx,
    kn, krm, val, o_early, m_early, l_early, ho, po, share, pair_in, sums_in,
    load_sem, xy_send, z_send, c_send, kb_recv,
    pair_send, pair_recv, sums_send, sums_recv,
):
    pool = lax.axis_index("pool")
    head = lax.axis_index("head")
    mx, my = pool // 4, pool % 4
    z, core = head // 2, head % 2
    zp = z % 2
    partner = z * 2 + (1 - core)

    def along_z(n):
        return lax.rem(z + NZ + n, NZ) * 2 + core

    zkey = lax.rem(z + 1 + core * (NZ - 2), NZ) * 2 + core

    def peer(o, way):
        dx, dy = OFFSETS[o]
        if o < OWN:
            way = way * (1 - 2 * zp)
        return ((mx + way * dx + 4) % 4) * 4 + (my + way * dy + 4) % 4

    loads = []

    def load(src, dst):
        copy = pltpu.make_async_copy(src, dst, load_sem.at[len(loads)])
        copy.start()
        loads.append(copy)
        return copy

    ld_pool_r = load(pool_rope, pool_r)
    ld_pool_l = load(pool_latent, pool_l)

    barrier = pltpu.get_barrier_semaphore()
    for o in range(SENT):
        if o != OWN:
            pl.semaphore_signal(barrier, inc=1, device_id=(peer(o, -1), head), device_id_type=MESH)
    for other in (partner, along_z(1), along_z(-1), along_z(2), along_z(-2)):
        pl.semaphore_signal(barrier, inc=1, device_id=(pool, other), device_id_type=MESH)

    ld_res_l = load(res_latent.at[0], loc_l.at[pl.ds(0, RES)])
    ld_new_l = load(new_latent, loc_l.at[pl.ds(RES, SUF)])
    ld_uk = load(w_uk, wuk)
    ld_uv = [load(w_uv.at[h], wuv.at[:, pl.ds(h * 128, 128)]) for h in range(HL)]
    ld_res_r = load(res_rope.at[0], loc_r.at[:, pl.ds(0, RES)])
    ld_new_r = load(new_rope, loc_r.at[:, pl.ds(RES, SUF)])
    ld_qr = load(q_rope, qr)
    ld_qn = load(q_nope, qn)
    ld_out = load(w_out, wout)

    low = pool * SLOTS
    slots = []
    for o in range(SENT):
        row = peer(o, 1)
        found = jnp.int32(0)
        for j in range(NBMAX):
            at = j + (1 - core) * (NBMAX - 1 - 2 * j)
            rel = table[row, at] - low
            found = jnp.where((rel >= 0) & (rel < SLOTS), rel, found)
        slots.append(found)

    pick_row = lax.broadcasted_iota(jnp.int32, (16, SLOTS), 0)
    pick_lane = lax.broadcasted_iota(jnp.int32, (16, SLOTS), 1)
    pick = jnp.zeros((16, SLOTS), f32)
    for o in range(SENT):
        pick = jnp.where((pick_row == o) & (pick_lane == slots[o]), 1.0, pick)
    ld_pool_r.wait()
    chosen = dot(pick.astype(bf16), pool_r[...])
    for r in range(32):
        rope_f[pl.ds(r, 16, stride=32), :] = chosen[:, r * 128 : r * 128 + 128]
    ld_pool_l.wait()
    for o in range(SENT):
        block = pool_l[slots[o]]
        for j in range(4):
            send_buf[o, j * BLK : (j + 1) * BLK, :] = block[:, j * 128 : j * 128 + 128]
        send_buf[o, LAT:MSG, :] = rope_f[o * 32 : o * 32 + 32, :].astype(bf16)
    kb[0, OWN] = send_buf[OWN]

    pl.semaphore_wait(barrier, SENT - 1 + 5)

    def remote(src, dst, send, recv, device):
        return pltpu.make_async_remote_copy(
            src_ref=src, dst_ref=dst, send_sem=send, recv_sem=recv,
            device_id=device, device_id_type=MESH,
        )

    def xy(o):
        return remote(send_buf.at[o], kb.at[0, o], xy_send.at[o], kb_recv.at[0, o], (peer(o, 1), head))

    def over_z(o):
        return remote(kb.at[0, o], kb.at[0, SENT + o], z_send.at[o], kb_recv.at[0, SENT + o], (pool, zkey))

    def over_core(o):
        return remote(kb.at[0, o], kb.at[1, o], c_send.at[o], kb_recv.at[1, o], (pool, partner))

    def arrive(*which):
        for o in which:
            if o >= SENT:
                over_z(o - SENT).wait_recv()
            elif o != OWN:
                xy(o).wait_recv()
            if o < OWN:
                over_z(o).start()
            over_core(o).start()

    def arrive_core(*which):
        for o in which:
            over_core(o).wait_recv()

    def send(*which):
        for o in which:
            xy(o).start()

    def left(*which):
        for o in which:
            xy(o).wait_send()

    send(0, 1, 2, 4, 5, 6)
    over_core(OWN).start()

    group = lax.broadcasted_iota(jnp.int32, (16, 128), 0)
    lane = lax.broadcasted_iota(jnp.int32, (16, 128), 1)
    blk = 2 * group + lane // BLK
    turn = 7 - blk // 4
    b_c, b_o = turn % 2, (turn // 2) * 4 + blk % 4
    b_dx, b_dy = jnp.zeros_like(blk), jnp.zeros_like(blk)
    for o in range(16):
        dx, dy = OFFSETS[o] if o < SENT else OFFSETS[o - SENT]
        way = (1 - 2 * zp) if o < OWN else (2 * zp - 1) if o >= SENT else 1
        b_dx = jnp.where(b_o == o, dx * way, b_dx)
        b_dy = jnp.where(b_o == o, dy * way, b_dy)
    b_src = ((mx - b_dx + 4) % 4) * 4 + (my - b_dy + 4) % 4
    b_rank = (core + b_c) % 2
    b_low = b_src * SLOTS
    count = jnp.zeros((16, 128), jnp.int32)
    for j in range(NBMAX):
        listed = table[pool, j]
        count = count + jnp.where((listed >= b_low) & (listed < b_low + SLOTS), 1, 0)
    rest_bias = jnp.where(count > b_rank, 0.0, -BIG)
    first_row = lax.broadcasted_iota(jnp.int32, (64, 128), 0) == 0

    def put_bias(g, row):
        krm[64:128, g * 128 : (g + 1) * 128] = jnp.where(first_row, row, 0.0).astype(bf16)

    for g in range(16):
        put_bias(g, rest_bias[g : g + 1, :])
    lane1 = lax.broadcasted_iota(jnp.int32, (1, 128), 1)
    for g in range(4):
        limit = res_len[0] if g < 2 else suf_len[0]
        put_bias(16 + g, jnp.where(lane1 + (g % 2) * 128 < limit, 0.0, -BIG))

    def expand(lat, at, n):
        kn[:, at : at + n] = (
            lax.dot_general(
                wuk[...].reshape(HL * NOPE, KV), lat, (((1,), (1,)), ((), ())), preferred_element_type=f32
            )
            * FACTOR
        ).astype(bf16)
        val[at : at + n, :] = dot(lat, wuv[...]).astype(bf16)

    def expand_rest(rc, o):
        lat = jnp.concatenate(
            [kb[rc, o : o + 4, j * BLK : (j + 1) * BLK, :].reshape(4 * BLK, 128) for j in range(4)], axis=1
        )
        at = (7 - (o // 4 * 2 + rc)) * 4 * BLK
        expand(lat, at, 4 * BLK)
        for i in range(0, 4, 2):
            a = kb[rc, o + i, LAT:MSG, :].astype(f32) * FACTOR
            b = kb[rc, o + i + 1, LAT:MSG, :].astype(f32) * FACTOR
            even = jnp.concatenate([a[:, :BLK], b[:, :BLK]], axis=1)
            odd = jnp.concatenate([a[:, BLK:], b[:, BLK:]], axis=1)
            krm[0:64, at + i * BLK : at + (i + 2) * BLK] = jnp.concatenate([even, odd], axis=0).astype(bf16)

    t_row = lax.broadcasted_iota(jnp.int32, (SUF, SUF), 0)
    u_col = lax.broadcasted_iota(jnp.int32, (SUF, SUF), 1)

    def scores(rows, h, keys):
        q = jnp.concatenate([qn[rows, h * NOPE : (h + 1) * NOPE], qx[h, rows, :]], axis=1)
        k = jnp.concatenate([kn[h * NOPE : (h + 1) * NOPE, keys], krm[:, keys]], axis=0)
        return dot(q, k)

    early = slice(SPLIT, KEYS)
    late = slice(0, SPLIT)

    def early_scores(h):
        s = scores(slice(0, SUF), h, early)
        n = KEYS - SUF - SPLIT
        return jnp.concatenate([s[:, :n], jnp.where(u_col <= t_row, s[:, n:], -BIG)], axis=1)

    def attend_early(h, s):
        m = jnp.max(s, axis=1, keepdims=True)
        p = jnp.exp2(s - m)
        total = jnp.sum(p, axis=1, keepdims=True)
        o_early[h] = dot(p.astype(bf16), val[early, h * 128 : (h + 1) * 128])
        m_early[h] = jnp.broadcast_to(m, (SUF, 128))
        l_early[h] = jnp.broadcast_to(total, (SUF, 128))

    def attend(c, h, s):
        rows = slice(c * HALF, (c + 1) * HALF)
        m0 = m_early[h, rows, :]
        m = jnp.maximum(m0, jnp.max(s, axis=1, keepdims=True))
        old = jnp.exp2(m0 - m)
        p = jnp.exp2(s - m[:, 0:1])
        total = l_early[h, rows, :] * old + jnp.sum(p, axis=1, keepdims=True)
        o = o_early[h, rows, :] * old + dot(p.astype(bf16), val[late, h * 128 : (h + 1) * 128])
        ho[rows, h * 128 : (h + 1) * 128] = (o / total).astype(bf16)

    def early_heads(first, last):
        s = early_scores(first)
        for h in range(first, last):
            later = early_scores(h + 1) if h + 1 < last else None
            attend_early(h, s)
            s = later

    ld_res_l.wait()
    ld_uk.wait()
    for copy in ld_uv:
        copy.wait()
    expand(loc_l[0:RES, :], REST, RES)
    left(0, 1, 2)
    send(7, 8, 9)
    ld_new_l.wait()
    expand(loc_l[RES : RES + SUF, :], REST + RES, SUF)
    arrive(0, 1, 2)
    left(4, 5, 6)
    send(10, 11, 12)

    ld_res_r.wait()
    ld_new_r.wait()
    perm_r = lax.broadcasted_iota(jnp.int32, (64, 64), 0)
    perm_c = lax.broadcasted_iota(jnp.int32, (64, 64), 1)
    perm = jnp.where(perm_c == 2 * (perm_r % 32) + perm_r // 32, 1.0, 0.0).astype(bf16)
    krm[0:64, REST:KEYS] = (dot(perm, loc_r[...]) * FACTOR).astype(bf16)

    ld_qr.wait()
    ld_qn.wait()
    lane_r = lax.broadcasted_iota(jnp.int32, (128, 128), 0)
    lane_c = lax.broadcasted_iota(jnp.int32, (128, 128), 1)
    one_lane = lax.broadcasted_iota(jnp.int32, (SUF, 128), 1) == 64
    for h in range(HL):
        spread = jnp.where(
            (lane_c < 64) & (lane_r == (h % 2) * 64 + 2 * (lane_c % 32) + lane_c // 32), 1.0, 0.0
        ).astype(bf16)
        turned = dot(qr[:, (h // 2) * 128 : (h // 2) * 128 + 128], spread)
        qx[h] = jnp.where(one_lane, 1.0, turned).astype(bf16)

    expand_rest(0, 0)
    arrive(4, 5, 6, 7)
    arrive_core(0, 1, 2, OWN)
    expand_rest(1, 0)
    expand_rest(0, 4)
    early_heads(0, 2)
    arrive(8, 9, 10, 11, 12)
    arrive_core(4, 5, 6, 7)
    expand_rest(1, 4)
    expand_rest(0, 8)
    early_heads(2, 5)
    arrive(13, 14, 15)
    arrive_core(8, 9, 10, 11)
    expand_rest(1, 8)
    early_heads(5, 8)
    expand_rest(0, 12)
    arrive_core(12, 13, 14, 15)
    expand_rest(1, 12)

    zh = z // 2
    groups = (
        lax.rem(zh + 2, 4), lax.rem(zh + 1 + 2 * zp, 4), lax.rem(zh + 3 - 2 * zp, 4), zh,
    )

    def pair(c, i):
        two = pl.ds(groups[i] * 2, 2)
        return remote(
            share.at[c, 1, two], pair_in.at[c, two], pair_send.at[c, i], pair_recv.at[c, i], (pool, partner)
        )

    def hop(c, i):
        way = 1 - 2 * (c % 2)
        of, to = ((4, 2 * way), (3, 1), (-3, -1), (1, 1), (-1, -1), (2, 2), (-2, -2))[i]
        return remote(
            share.at[c, 0, lax.rem(z + NZ + of, NZ)], sums_in.at[c, i], sums_send.at[c, i],
            sums_recv.at[c, i], (pool, along_z(to)),
        )

    def add(c, of, *parts):
        k = lax.rem(z + NZ + of, NZ)
        total = share[c, 0, k].astype(f32)
        for part in parts:
            total = total + part.astype(f32)
        share[c, 0, k] = total.astype(bf16)

    def paired(c, *which):
        for of in which:
            add(c, of, pair_in[c, lax.rem(z + NZ + of, NZ)])

    def step1(c):
        pair(c, 0).wait_recv()
        pair(c, 1).wait_recv()
        paired(c, 4, 3, -3)
        for i in range(3):
            hop(c, i).start()
        pair(c, 2).wait_recv()
        pair(c, 3).wait_recv()
        paired(c, 1, -1)
        for i in range(3, 5):
            hop(c, i).start()
        paired(c, 2, -2, 0)

    def step2(c):
        for i in range(3):
            hop(c, i).wait_recv()
        if c % 2 == 0:
            add(c, 2, sums_in[c, 0], sums_in[c, 1])
            add(c, -2, sums_in[c, 2])
        else:
            add(c, 2, sums_in[c, 1])
            add(c, -2, sums_in[c, 0], sums_in[c, 2])
        for i in range(5, 7):
            hop(c, i).start()

    def finish(c):
        for i in range(3, 7):
            hop(c, i).wait_recv()
        total = share[c, 0, z].astype(f32)
        for i in range(3, 7):
            total = total + sums_in[c, i].astype(f32)
        tall = jnp.concatenate([total[:, g * COLS : (g + 1) * COLS] for g in range(4)], axis=0)
        rows = lax.broadcasted_iota(jnp.int32, (HALF, COLS), 0) + c * HALF
        out[:, c * HALF : (c + 1) * HALF] = jnp.where(rows < suf_len[0], tall, 0.0).T.astype(bf16)

    for c in range(CHUNKS):
        rows = slice(c * HALF, (c + 1) * HALF)
        s = scores(rows, 0, late)
        for h in range(HL):
            later = scores(rows, h + 1, late) if h + 1 < HL else None
            attend(c, h, s)
            s = later
            if c > 0 and h == 4:
                step1(c - 1)
        if c == 0:
            ld_out.wait()
        for n in range(0, DW, 512):
            po[:, n : n + 512] = dot(ho[c * HALF : (c + 1) * HALF, :], wout[:, n : n + 512]).astype(bf16)
        for i in range(4):
            g = groups[i]
            part = po[:, pl.ds(pl.multiple_of(g * (4 * COLS), 128), 4 * COLS)]
            for k in range(2):
                for cc in range(2):
                    at = (2 * k + cc) * COLS
                    share[c, (core + cc) % 2, 2 * g + k] = jnp.concatenate(
                        [part[n * PR : (n + 1) * PR, at : at + COLS] for n in range(4)], axis=1
                    )
            pair(c, i).start()
    step1(1)
    step2(0)
    step2(1)
    finish(0)
    finish(1)

    left(7, 8, 9, 10, 11, 12)
    for o in range(OWN):
        over_z(o).wait_send()
    for o in range(16):
        over_core(o).wait_send()
    for c in range(CHUNKS):
        for i in range(4):
            pair(c, i).wait_send()
        for i in range(7):
            hop(c, i).wait_send()


def body(*args):
    dma = pltpu.SemaphoreType.DMA
    vmem = lambda *shape, dtype=bf16: pltpu.VMEM(shape, dtype)
    anywhere = pl.BlockSpec(memory_space=pl.ANY)
    smem = pl.BlockSpec(memory_space=pltpu.SMEM)
    return pl.pallas_call(
        kernel,
        out_shape=jax.ShapeDtypeStruct((COLS, SUF), bf16),
        in_specs=[anywhere] * 8 + [smem] * 3 + [anywhere] * 3,
        out_specs=pl.BlockSpec(memory_space=pltpu.VMEM),
        scratch_shapes=[
            vmem(SLOTS, BLK, KV),
            vmem(SLOTS, ROPE * BLK),
            vmem(16 * 32, 128, dtype=f32),
            vmem(SENT, MSG, 128),
            vmem(2, 16, MSG, 128),
            vmem(RES + SUF, KV),
            vmem(ROPE, RES + SUF),
            vmem(HL, NOPE, KV),
            vmem(KV, HL * 128),
            vmem(HL * 128, DW),
            vmem(SUF, HL * NOPE),
            vmem(SUF, HL * ROPE),
            vmem(HL, SUF, 128),
            vmem(HL * NOPE, KEYS),
            vmem(128, KEYS),
            vmem(KEYS, HL * 128),
            vmem(HL, SUF, 128, dtype=f32),
            vmem(HL, SUF, 128, dtype=f32),
            vmem(HL, SUF, 128, dtype=f32),
            vmem(SUF, HL * 128),
            vmem(HALF, DW),
            vmem(CHUNKS, 2, NZ, PR, 4 * COLS),
            vmem(CHUNKS, NZ, PR, 4 * COLS),
            vmem(CHUNKS, 7, PR, 4 * COLS),
            dma((20,)), dma((SENT,)), dma((OWN,)), dma((16,)), dma((2, 16)),
            dma((CHUNKS, 4)), dma((CHUNKS, 4)), dma((CHUNKS, 7)), dma((CHUNKS, 7)),
        ],
        compiler_params=pltpu.CompilerParams(
            collective_id=0, has_side_effects=True, vmem_limit_bytes=60 * 2**20
        ),
        cost_estimate=pl.CostEstimate(flops=12 * 10**9, bytes_accessed=14 * 10**6, transcendentals=5 * 10**6),
    )(*args).T


def solution(mesh):
    placed = (
        P("pool", "head"), P("pool", "head"), P("pool", None), P(None, "pool"),
        P("pool", None, None), P("pool", None, None), P("pool", None, None), P("pool", None),
        P(), P("pool"), P("pool"),
        P("head", None, None), P("head", None, None), P("head", None),
    )
    return jax.shard_map(
        body, mesh=mesh, in_specs=placed, out_specs=P("pool", "head"), check_vma=False
    )
```
